512 devices in a mesh: patch: 32 (over y_lo, z), head: 8 (over y_hi, x), cfg: 2 (over core).
Axes of the slice: x: 4, y: 4 (y_hi: 2, y_lo: 2; y = y_hi * 2 + y_lo), z: 16, core: 2. Of those that a mesh axis runs over, the one named last changes fastest.
Arguments:
- qkv: bfloat16 [2, 3, 8192, 3072], P('cfg', None, ('patch', 'head')), may hold values from -45 to 45
- stale_kv: bfloat16 [2, 2, 8192, 3072], P('cfg', None, 'patch', 'head'), may hold values from -10 to 10
- tokens_in: bfloat16 [8192, 3072], P(('patch', 'head'), 'cfg'), may hold values from -6 to 6
- out_weight: bfloat16 [3072, 3072], P('head'), may hold values from -0.109375 to 0.109375
- gate: float32 [3072], P('cfg'), may hold values from 0.1 to 1.9
Outputs:
- next_kv: bfloat16 [2, 2, 8192, 3072], P('cfg', None, 'patch', 'head')
- guided: bfloat16 [8192, 3072], P(('patch', 'head'), 'cfg')
The draws below stay inside these ranges and needn't reach their ends.
All inputs are finite; a program needn't handle non-finite values.
Results may differ from the reference program's by a relative error of at most 0.019.
Values may be sent and summed in bfloat16 or wider, within the bound.
A program may use at most 64 MiB of HBM per device.

```python
import jax
import jax.numpy as jnp
from jax import lax

D = 3072
HEADS = 24
HD = 128
TOK_DEV = 32
TOKENS = 8192
N_PATCH = 32
N_HEAD = 8


def stale_common(key):
    key = jax.random.fold_in(key, 29)
    return jnp.clip(jax.random.normal(key, (2, 2, TOKENS, D), jnp.float32) * 1.7, -10.0, 10.0)


def draw_stale_kv(key, part):
    shared = stale_common(key)
    full = shared
    return full.astype(jnp.bfloat16)


def draw_qkv(key, part):
    key = jax.random.fold_in(key, 11)
    base_scale = 1.7
    full = jnp.clip(jax.random.normal(key, (2, 3, TOKENS, D), jnp.float32), -6.0, 6.0) * base_scale
    return full.astype(jnp.bfloat16)


def block_levels(stream_key, extent, pieces, low, largest):
    factor_of = 1.0
    for position, parts in pieces:
        draws = jax.random.uniform(jax.random.fold_in(jax.random.fold_in(stream_key, 6), position), (parts,), jnp.float32, low / len(pieces), largest / len(pieces))
        factor_of = factor_of * jnp.repeat(jnp.exp(draws), extent[position] // parts).reshape((-1,) + (1,) * (len(extent) - 1 - position))
    return factor_of


def gaussian(own_key, dims, scale, reach, split=(), kind=jnp.bfloat16):
    loudness = block_levels(own_key, dims, split, -0.22, 0.18) if split else 1.0
    drawn = jax.random.normal(own_key, dims, jnp.float32) * scale * loudness
    return jnp.minimum(jnp.maximum(drawn, -reach), reach).astype(kind)


def setup_inputs(seed: int = 0) -> dict:
    streams_of = jax.random.split(jax.random.key(seed), 6)
    qkv = draw_qkv(jax.random.fold_in(streams_of[5], 71), 0)
    stale_kv = draw_stale_kv(jax.random.fold_in(streams_of[5], 71), 0)
    tokens_in = gaussian(streams_of[2], (TOKENS, D), 1.0, 6.0, ((0, 256), (1, 2)))
    out_weight = gaussian(streams_of[3], (D, D), D ** -0.5, 0.109375, ((0, 8),))
    gate = jnp.clip(1.0 + 0.18 * jax.random.normal(streams_of[4], (D,), jnp.float32), 0.1, 1.9)
    return dict(qkv=qkv, stale_kv=stale_kv, tokens_in=tokens_in, out_weight=out_weight, gate=gate)


guide_scale = 6.0


def attend_patch(queries, keys, values):
    scores = jnp.einsum('qhd,khd->hqk', queries.astype(jnp.float32), keys.astype(jnp.float32)) * (HD ** -0.5)
    maxima = jnp.max(scores, axis=-1, keepdims=True)
    weights = jnp.exp(scores - maxima)
    totals = jnp.sum(weights, axis=-1)
    rounded = lax.optimization_barrier(weights.astype(jnp.bfloat16))
    summed = jnp.einsum('hqk,khd->hqd', rounded.astype(jnp.float32), values.astype(jnp.float32))
    return (summed / totals[..., None]).astype(jnp.bfloat16)


def reference(qkv, stale_kv, tokens_in, out_weight, gate):
    rows = TOK_DEV * N_HEAD
    projected = []
    for branch in range(2):
        def one_patch(index):
            start = (index * rows).astype(jnp.int32)
            queries = lax.dynamic_slice_in_dim(qkv[branch, 0], start, rows, 0).reshape(rows, HEADS, HD)
            fresh_keys = lax.dynamic_slice_in_dim(qkv[branch, 1], start, rows, 0)
            fresh_values = lax.dynamic_slice_in_dim(qkv[branch, 2], start, rows, 0)
            keys = lax.dynamic_update_slice_in_dim(stale_kv[branch, 0], fresh_keys, start, 0).reshape(TOKENS, HEADS, HD)
            values = lax.dynamic_update_slice_in_dim(stale_kv[branch, 1], fresh_values, start, 0).reshape(TOKENS, HEADS, HD)
            result = attend_patch(queries, keys, values)
            return jnp.transpose(result, (1, 0, 2)).reshape(rows, D)
        attended = lax.map(one_patch, jnp.arange(N_PATCH, dtype=jnp.int32)).reshape(TOKENS, D)
        projected.append(jnp.dot(attended, out_weight, preferred_element_type=jnp.float32))
    mixed = guide_scale * projected[0] - (guide_scale - 1.0) * projected[1]
    guided = (tokens_in.astype(jnp.float32) + gate * mixed).astype(jnp.bfloat16)
    return qkv[:, 1:3], guided
```

```python
import functools
import math

import jax
import jax.numpy as jnp
from jax import lax
from jax.experimental import pallas as pl
from jax.experimental.pallas import tpu as pltpu
from jax.sharding import PartitionSpec as P

HD = 128
GUIDE = 6.0
MESH = pl.DeviceIdType.MESH
BF16 = jnp.bfloat16
F32 = jnp.float32
SCALE2 = HD ** (-0.5) * math.log2(math.e)


def kernel(
    nz,
    nh,
    qkv_ref,
    stale_ref,
    tokens_ref,
    weight_ref,
    gate_ref,
    next_ref,
    guided_ref,
    fresh,
    own,
    kv,
    far,
    qc,
    qpart,
    maxima,
    totals,
    summed,
    part_out,
    part_in,
    stat_out,
    stat_in,
    att,
    att_other,
    mixed,
    weight,
    tokens,
    gate,
    rs_out,
    rs_in,
    ring_send,
    ring_recv,
    a2a_send,
    a2a_recv,
    part_send,
    part_recv,
    cfg_send,
    cfg_recv,
    rs_send,
    rs_recv,
    local_sem,
):
    tok = qkv_ref.shape[2]
    rows = tok * nh
    width = stale_ref.shape[3]
    count = width // HD
    half = tokens_ref.shape[1]
    nfull = nz // 2 - 1
    patch = lax.axis_index("patch")
    head = lax.axis_index("head")
    cfg = lax.axis_index("cfg")
    column = patch // nz
    z = lax.rem(patch, nz)
    ahead = {"patch": column * nz + lax.rem(z + 1, nz)}
    behind = {"patch": column * nz + lax.rem(z + nz - 1, nz)}
    partner = {"patch": lax.rem(patch + nz, 2 * nz)}
    other = {"cfg": 1 - cfg}
    around = (ahead, behind)
    peers = [{"head": lax.rem(head + i, nh)} for i in range(1, nh)]

    def remote(src, dst, send, recv, device):
        return pltpu.make_async_remote_copy(
            src_ref=src,
            dst_ref=dst,
            send_sem=send,
            recv_sem=recv,
            device_id=device,
            device_id_type=MESH,
        )

    def ring_first(k, side):
        return remote(
            stale_ref.at[0, :, :, pl.ds(k * HD, HD)],
            kv.at[0, k, :, side],
            ring_send.at[side, 0, k],
            ring_recv.at[side, 0, k],
            around[side],
        )

    def ring_next(slot, k, side):
        return remote(
            kv.at[slot - 1, k, :, side],
            kv.at[slot, k, :, side],
            ring_send.at[side, slot, k],
            ring_recv.at[side, slot, k],
            around[side],
        )

    def ring_far(k, side):
        return remote(
            kv.at[nfull - 1, k, side, side],
            far.at[k, side],
            ring_send.at[side, nfull, k],
            ring_recv.at[side, nfull, k],
            around[side],
        )

    def arrived(slot, k, side):
        remote(
            kv.at[slot, k, :, side],
            kv.at[slot, k, :, side],
            ring_send.at[side, slot, k],
            ring_recv.at[side, slot, k],
            around[side],
        ).wait_recv()

    def a2a_to(i):
        target = lax.rem(head + i, nh)
        return remote(
            qkv_ref.at[0, :, :, pl.ds(pl.multiple_of(target * width, HD), width)],
            fresh.at[:, pl.ds(pl.multiple_of(head * tok, tok), tok)],
            a2a_send.at[i],
            a2a_recv.at[i],
            peers[i - 1],
        )

    own_copy = pltpu.make_async_copy(stale_ref.at[0], own, local_sem.at[0])
    mine_copy = pltpu.make_async_copy(
        qkv_ref.at[0, :, :, pl.ds(pl.multiple_of(head * width, HD), width)],
        fresh.at[:, pl.ds(pl.multiple_of(head * tok, tok), tok)],
        local_sem.at[1],
    )
    weight_copy = pltpu.make_async_copy(
        weight_ref.at[:, pl.ds(pl.multiple_of(cfg * half, HD), half)], weight, local_sem.at[2]
    )
    tokens_copy = pltpu.make_async_copy(tokens_ref, tokens, local_sem.at[3])
    gate_copy = pltpu.make_async_copy(gate_ref, gate, local_sem.at[4])
    next_copy = pltpu.make_async_copy(fresh.at[pl.ds(1, 2)], next_ref.at[0], local_sem.at[5])

    barrier = pltpu.get_barrier_semaphore()
    greeted = [ahead, behind, partner, other] + peers
    for device in greeted:
        pl.semaphore_signal(barrier, inc=1, device_id=device, device_id_type=MESH)
    own_copy.start()
    mine_copy.start()
    weight_copy.start()
    tokens_copy.start()
    gate_copy.start()
    pl.semaphore_wait(barrier, len(greeted))

    for k in range(count):
        for side in range(2):
            ring_first(k, side).start()
    for i in range(1, nh):
        a2a_to(i).start()

    def pass_on(slot):
        for k in range(count):
            for side in range(2):
                arrived(slot, k, side)
                if isinstance(slot, int) and slot == nfull - 1:
                    ring_far(k, side).start()
                else:
                    ring_next(slot + 1, k, side).start()

    def attend(k, start, size, keys, values, first=False):
        span = pl.ds(start, size)
        scores = lax.dot_general(
            qc[k, span], keys, (((1,), (1,)), ((), ())), preferred_element_type=F32
        )
        block_max = jnp.max(scores, axis=1, keepdims=True)
        if first:
            new_max = jnp.broadcast_to(block_max, (size, HD))
        else:
            old_max = maxima[k, span]
            new_max = jnp.maximum(old_max, block_max)
            factor = jnp.exp2((old_max - new_max) * SCALE2)
        lanes = [
            jnp.exp2((scores[:, j : j + HD] - new_max) * SCALE2)
            for j in range(0, scores.shape[1], HD)
        ]
        total = functools.reduce(jnp.add, lanes)
        weights = jnp.concatenate([lane.astype(BF16) for lane in lanes], axis=1)
        product = jnp.dot(weights, values, preferred_element_type=F32)
        maxima[k, span] = new_max
        if first:
            totals[k, span] = total
            summed[k, span] = product
        else:
            totals[k, span] = totals[k, span] * factor + total
            summed[k, span] = summed[k, span] * factor + product

    def attend_slot(slot, k):
        keys = kv[slot, k, 0].reshape(2 * rows, HD)
        values = kv[slot, k, 1].reshape(2 * rows, HD)
        for start in (0, rows):
            attend(k, start, rows, keys, values)

    early = min(2, nfull)
    pass_on(0)
    mine_copy.wait()
    for i in range(1, nh):
        a2a_to(i).wait_recv()
    next_copy.start()
    query_copy = remote(
        fresh.at[0], qpart, part_send.at[0, count], part_recv.at[0, count], partner
    )
    query_copy.start()
    for k in range(count):
        qc[k, 0:rows] = fresh[0, :, k * HD : (k + 1) * HD]
    for slot in range(1, early):
        pass_on(slot)
    own_copy.wait()
    query_copy.wait_recv()
    for k in range(count):
        columns = slice(k * HD, (k + 1) * HD)
        qc[k, rows : 2 * rows] = qpart[:, columns]
        attend(k, 0, rows, fresh[1, :, columns], fresh[2, :, columns], first=True)
        attend(k, rows, rows, own[0, :, columns], own[1, :, columns], first=True)
        for slot in range(early):
            attend_slot(slot, k)

    def step(slot, carry):
        for k in range(count):
            for side in range(2):
                arrived(slot, k, side)
                ring_next(slot + 1, k, side).start()
            attend_slot(slot, k)
        return carry

    if nfull > early:
        lax.fori_loop(early, nfull - 1, step, 0)
        for k in range(count):
            for side in range(2):
                arrived(nfull - 1, k, side)
                ring_far(k, side).start()
            attend_slot(nfull - 1, k)

    def part_copy(k):
        return remote(
            part_out.at[k], part_in.at[k], part_send.at[0, k], part_recv.at[0, k], partner
        )

    def stat_copy(k):
        return remote(
            stat_out.at[k], stat_in.at[k], part_send.at[1, k], part_recv.at[1, k], partner
        )

    def cfg_copy(k):
        return remote(att.at[k], att_other.at[k], cfg_send.at[k], cfg_recv.at[k], other)

    lane = lax.broadcasted_iota(jnp.int32, (rows, HD), 1)
    for k in range(count):
        for side in range(2):
            ring_far(k, side).wait_recv()
        for start in (rows, 0):
            attend(k, start, rows, far[k, 0], far[k, 1])
        part_out[k] = summed[k, rows : 2 * rows].astype(BF16)
        total = jnp.sum(totals[k, rows : 2 * rows], axis=1, keepdims=True)
        stats = jnp.where(lane < HD // 2, maxima[k, rows : 2 * rows], total)
        stat_out[k] = jnp.transpose(stats)[HD // 2 - 8 : HD // 2 + 8]
        part_copy(k).start()
        stat_copy(k).start()

    for k in range(count):
        part_copy(k).wait_recv()
        stat_copy(k).wait_recv()
        max_here = maxima[k, 0:rows]
        total_here = jnp.sum(totals[k, 0:rows], axis=1, keepdims=True)
        max_there = jnp.transpose(jnp.broadcast_to(stat_in[k, 0:1], (HD, rows)))
        total_there = jnp.transpose(jnp.broadcast_to(stat_in[k, 8:9], (HD, rows)))
        top = jnp.maximum(max_here, max_there)
        keep = jnp.exp2((max_here - top) * SCALE2)
        add = jnp.exp2((max_there - top) * SCALE2)
        total = total_here * keep + total_there * add
        value = summed[k, 0:rows] * keep + part_in[k].astype(F32) * add
        att[k] = (value / total).astype(BF16)
        cfg_copy(k).start()

    weight_copy.wait()
    mine = jnp.where(cfg == 0, GUIDE, 1.0 - GUIDE)
    theirs = jnp.where(cfg == 0, 1.0 - GUIDE, GUIDE)
    for k in range(count):
        cfg_copy(k).wait_recv()
        mixed[:, k * HD : (k + 1) * HD] = (
            mine * att[k].astype(F32) + theirs * att_other[k].astype(F32)
        ).astype(BF16)

    piece = 512 if half % 512 == 0 else half

    def project(j, carry):
        columns = pl.ds(pl.multiple_of(j * piece, HD), piece)
        block = jnp.dot(mixed[...], weight[:, columns], preferred_element_type=F32)
        rs_out[:, :, columns] = block.astype(BF16).reshape(nh, tok, piece)
        return carry

    lax.fori_loop(0, half // piece, project, 0)

    def rs_copy(i):
        return remote(
            rs_out.at[lax.rem(head + i, nh)],
            rs_in.at[i],
            rs_send.at[i],
            rs_recv.at[i],
            peers[i - 1],
        )

    for i in range(1, nh):
        rs_copy(i).start()
    tokens_copy.wait()
    gate_copy.wait()
    for i in range(1, nh):
        rs_copy(i).wait_recv()

    def finish(j, carry):
        columns = pl.ds(pl.multiple_of(j * piece, HD), piece)
        value = rs_out[head, :, columns].astype(F32)
        for i in range(1, nh):
            value = value + rs_in[i, :, columns].astype(F32)
        guided_ref[:, columns] = (
            tokens[:, columns].astype(F32) + gate[:, columns] * value
        ).astype(BF16)
        return carry

    lax.fori_loop(0, half // piece, finish, 0)

    next_copy.wait()
    query_copy.wait_send()
    for k in range(count):
        for side in range(2):
            ring_first(k, side).wait_send()
            ring_far(k, side).wait_send()
        part_copy(k).wait_send()
        stat_copy(k).wait_send()
        cfg_copy(k).wait_send()

    def sent(slot, carry):
        for k in range(count):
            for side in range(2):
                ring_next(slot, k, side).wait_send()
        return carry

    lax.fori_loop(1, nfull, sent, 0)
    for i in range(1, nh):
        a2a_to(i).wait_send()
        rs_copy(i).wait_send()


def solution(mesh):
    nz = mesh.shape["patch"] // 2
    nh = mesh.shape["head"]

    def body(qkv, stale_kv, tokens_in, out_weight, gate):
        tok = qkv.shape[2]
        rows = tok * nh
        width = stale_kv.shape[3]
        count = width // HD
        half = tokens_in.shape[1]
        nfull = nz // 2 - 1
        anywhere = pl.BlockSpec(memory_space=pl.ANY)
        dma = pltpu.SemaphoreType.DMA
        return pl.pallas_call(
            functools.partial(kernel, nz, nh),
            out_shape=(
                jax.ShapeDtypeStruct((1, 2, rows, width), BF16),
                jax.ShapeDtypeStruct((tok, half), BF16),
            ),
            in_specs=[anywhere] * 5,
            out_specs=(anywhere, pl.BlockSpec(memory_space=pltpu.VMEM)),
            scratch_shapes=[
                pltpu.VMEM((3, rows, width), BF16),
                pltpu.VMEM((2, rows, width), BF16),
                pltpu.VMEM((nfull, count, 2, 2, rows, HD), BF16),
                pltpu.VMEM((count, 2, rows, HD), BF16),
                pltpu.VMEM((count, 2 * rows, HD), BF16),
                pltpu.VMEM((rows, width), BF16),
                pltpu.VMEM((count, 2 * rows, HD), F32),
                pltpu.VMEM((count, 2 * rows, HD), F32),
                pltpu.VMEM((count, 2 * rows, HD), F32),
                pltpu.VMEM((count, rows, HD), BF16),
                pltpu.VMEM((count, rows, HD), BF16),
                pltpu.VMEM((count, 16, rows), F32),
                pltpu.VMEM((count, 16, rows), F32),
                pltpu.VMEM((count, rows, HD), BF16),
                pltpu.VMEM((count, rows, HD), BF16),
                pltpu.VMEM((rows, width), BF16),
                pltpu.VMEM((width, half), BF16),
                pltpu.VMEM((tok, half), BF16),
                pltpu.VMEM((1, half), F32),
                pltpu.VMEM((nh, tok, half), BF16),
                pltpu.VMEM((nh, tok, half), BF16),
                dma((2, nfull + 1, count)),
                dma((2, nfull + 1, count)),
                dma((nh,)),
                dma((nh,)),
                dma((2, count + 1)),
                dma((2, count + 1)),
                dma((count,)),
                dma((count,)),
                dma((nh,)),
                dma((nh,)),
                dma((6,)),
            ],
            compiler_params=pltpu.CompilerParams(
                collective_id=0, has_side_effects=True, vmem_limit_bytes=40 * 1024 * 1024
            ),
        )(qkv, stale_kv, tokens_in, out_weight, gate.reshape(1, half))

    in_specs = (
        P("cfg", None, ("patch", "head"), None),
        P("cfg", None, "patch", "head"),
        P(("patch", "head"), "cfg"),
        P("head", None),
        P("cfg"),
    )
    out_specs = (P("cfg", None, "patch", "head"), P(("patch", "head"), "cfg"))
    return jax.shard_map(body, mesh=mesh, in_specs=in_specs, out_specs=out_specs, check_vma=False)
```

```python
import functools
import math

import jax
import jax.numpy as jnp
from jax import lax
from jax.experimental import pallas as pl
from jax.experimental.pallas import tpu as pltpu
from jax.sharding import PartitionSpec as P

HD = 128
GUIDE = 6.0
MESH = pl.DeviceIdType.MESH
BF16 = jnp.bfloat16
F32 = jnp.float32
WINDOW = 2
SCALE2 = HD ** (-0.5) * math.log2(math.e)


def kernel(
    nz,
    nh,
    qkv_ref,
    stale_ref,
    tokens_ref,
    weight_ref,
    gate_ref,
    next_ref,
    guided_ref,
    fresh,
    own,
    kv,
    far,
    qc,
    qpart,
    maxima,
    totals,
    summed,
    part_out,
    part_in,
    stat_out,
    stat_in,
    att,
    att_other,
    mixed,
    weight,
    tokens,
    gate,
    rs_out,
    rs_in,
    ring_send,
    ring_recv,
    a2a_send,
    a2a_recv,
    part_send,
    part_recv,
    cfg_send,
    cfg_recv,
    rs_send,
    rs_recv,
    local_sem,
):
    tok = qkv_ref.shape[2]
    rows = tok * nh
    width = stale_ref.shape[3]
    count = width // HD
    half = tokens_ref.shape[1]
    nfull = nz // 2 - 1
    patch = lax.axis_index("patch")
    head = lax.axis_index("head")
    cfg = lax.axis_index("cfg")
    column = patch // nz
    z = lax.rem(patch, nz)
    ahead = {"patch": column * nz + lax.rem(z + 1, nz)}
    behind = {"patch": column * nz + lax.rem(z + nz - 1, nz)}
    partner = {"patch": lax.rem(patch + nz, 2 * nz)}
    other = {"cfg": 1 - cfg}
    around = (ahead, behind)
    peers = [{"head": lax.rem(head + i, nh)} for i in range(1, nh)]

    def remote(src, dst, send, recv, device):
        return pltpu.make_async_remote_copy(
            src_ref=src,
            dst_ref=dst,
            send_sem=send,
            recv_sem=recv,
            device_id=device,
            device_id_type=MESH,
        )

    block = 2 * count
    last = nfull * block

    def ring_own(n, side):
        k, part = n // 2, n % 2
        return remote(
            stale_ref.at[0, part, :, pl.ds(k * HD, HD)],
            kv.at[k, part, side],
            ring_send.at[side, n],
            ring_recv.at[side, n],
            around[side],
        )

    def ring_next(u, part, side):
        return remote(
            kv.at[u - count, part, side],
            kv.at[u, part, side],
            ring_send.at[side, 2 * u + part],
            ring_recv.at[side, 2 * u + part],
            around[side],
        )

    def ring_far(k, side):
        return remote(
            kv.at[(nfull - 1) * count + k, side, side],
            far.at[k, side],
            ring_send.at[side, last + k],
            ring_recv.at[side, last + k],
            around[side],
        )

    def chunk(n, side):
        return remote(
            far.at[0, side],
            far.at[0, side],
            ring_send.at[side, n],
            ring_recv.at[side, n],
            around[side],
        )

    def a2a_to(i):
        target = lax.rem(head + i, nh)
        return remote(
            qkv_ref.at[0, :, :, pl.ds(pl.multiple_of(target * width, HD), width)],
            fresh.at[:, pl.ds(pl.multiple_of(head * tok, tok), tok)],
            a2a_send.at[i],
            a2a_recv.at[i],
            peers[i - 1],
        )

    own_copy = pltpu.make_async_copy(stale_ref.at[0], own, local_sem.at[0])
    mine_copy = pltpu.make_async_copy(
        qkv_ref.at[0, :, :, pl.ds(pl.multiple_of(head * width, HD), width)],
        fresh.at[:, pl.ds(pl.multiple_of(head * tok, tok), tok)],
        local_sem.at[1],
    )
    weight_copy = pltpu.make_async_copy(
        weight_ref.at[:, pl.ds(pl.multiple_of(cfg * half, HD), half)], weight, local_sem.at[2]
    )
    tokens_copy = pltpu.make_async_copy(tokens_ref, tokens, local_sem.at[3])
    gate_copy = pltpu.make_async_copy(gate_ref, gate, local_sem.at[4])
    next_copy = pltpu.make_async_copy(fresh.at[pl.ds(1, 2)], next_ref.at[0], local_sem.at[5])

    barrier = pltpu.get_barrier_semaphore()
    greeted = [ahead, behind, partner, other] + peers
    for device in greeted:
        pl.semaphore_signal(barrier, inc=1, device_id=device, device_id_type=MESH)
    own_copy.start()
    mine_copy.start()
    weight_copy.start()
    tokens_copy.start()
    gate_copy.start()
    pl.semaphore_wait(barrier, len(greeted))

    for n in range(block):
        for side in range(2):
            if n >= WINDOW:
                chunk(n - WINDOW, side).wait_send()
            ring_own(n, side).start()
        if n == min(WINDOW, block) - 1:
            for i in range(1, nh):
                a2a_to(i).start()

    def pass_on(u):
        for part in range(2):
            n = 2 * u + part
            for side in range(2):
                chunk(n - block, side).wait_recv()
                chunk(n - WINDOW, side).wait_send()
                ring_next(u, part, side).start()

    def attend(k, start, size, keys, values, first=False):
        span = pl.ds(start, size)
        scores = lax.dot_general(
            qc[k, span], keys, (((1,), (1,)), ((), ())), preferred_element_type=F32
        )
        block_max = jnp.max(scores, axis=1, keepdims=True)
        if first:
            new_max = jnp.broadcast_to(block_max, (size, HD))
        else:
            old_max = maxima[k, span]
            new_max = jnp.maximum(old_max, block_max)
            factor = jnp.exp2((old_max - new_max) * SCALE2)
        lanes = [
            jnp.exp2((scores[:, j : j + HD] - new_max) * SCALE2)
            for j in range(0, scores.shape[1], HD)
        ]
        total = functools.reduce(jnp.add, lanes)
        weights = jnp.concatenate([lane.astype(BF16) for lane in lanes], axis=1)
        product = jnp.dot(weights, values, preferred_element_type=F32)
        maxima[k, span] = new_max
        if first:
            totals[k, span] = total
            summed[k, span] = product
        else:
            totals[k, span] = totals[k, span] * factor + total
            summed[k, span] = summed[k, span] * factor + product

    def attend_chunk(v):
        k = lax.rem(v, count)
        keys = kv[v, 0].reshape(2 * rows, HD)
        values = kv[v, 1].reshape(2 * rows, HD)
        for start in (0, rows):
            attend(k, start, rows, keys, values)

    def loop(low, high, work):
        def step(i, carry):
            work(i)
            return carry

        lax.fori_loop(low, high, step, 0)

    chunks = nfull * count
    begin = min(3 * count, chunks)
    loop(count, min(2 * count, chunks), pass_on)
    mine_copy.wait()
    for i in range(1, nh):
        a2a_to(i).wait_recv()
    query_copy = remote(
        fresh.at[0], qpart, part_send.at[0, count], part_recv.at[0, count], partner
    )
    query_copy.start()
    next_copy.start()
    for k in range(count):
        qc[k, 0:rows] = fresh[0, :, k * HD : (k + 1) * HD]
    loop(min(2 * count, chunks), begin, pass_on)
    own_copy.wait()
    query_copy.wait_recv()
    for k in range(count):
        columns = slice(k * HD, (k + 1) * HD)
        qc[k, rows : 2 * rows] = qpart[:, columns]
        attend(k, 0, rows, fresh[1, :, columns], fresh[2, :, columns], first=True)
        attend(k, rows, rows, own[0, :, columns], own[1, :, columns], first=True)

    double = max(0, min(chunks - begin, begin - count))

    def catch_up(i):
        pass_on(begin + i)
        loop(2 * i, 2 * i + 2, attend_chunk)

    def follow(u):
        pass_on(u)
        attend_chunk(u - count)

    loop(0, double, catch_up)
    loop(begin + double, chunks, follow)
    done = 2 * double + max(0, chunks - begin - double)
    loop(done, chunks - count, attend_chunk)
    for k in range(count):
        u = chunks - count + k
        for side in range(2):
            for part in range(2):
                chunk(2 * u + part, side).wait_recv()
            chunk(last + k - WINDOW, side).wait_send()
            ring_far(k, side).start()
        attend_chunk(u)

    def part_copy(k):
        return remote(
            part_out.at[k], part_in.at[k], part_send.at[0, k], part_recv.at[0, k], partner
        )

    def stat_copy(k):
        return remote(
            stat_out.at[k], stat_in.at[k], part_send.at[1, k], part_recv.at[1, k], partner
        )

    def cfg_copy(k):
        return remote(att.at[k], att_other.at[k], cfg_send.at[k], cfg_recv.at[k], other)

    lane = lax.broadcasted_iota(jnp.int32, (rows, HD), 1)
    for k in range(count):
        for side in range(2):
            ring_far(k, side).wait_recv()
        for start in (rows, 0):
            attend(k, start, rows, far[k, 0], far[k, 1])
        part_out[k] = summed[k, rows : 2 * rows].astype(BF16)
        total = jnp.sum(totals[k, rows : 2 * rows], axis=1, keepdims=True)
        stats = jnp.where(lane < HD // 2, maxima[k, rows : 2 * rows], total)
        stat_out[k] = jnp.transpose(stats)[HD // 2 - 8 : HD // 2 + 8]
        part_copy(k).start()
        stat_copy(k).start()

    for k in range(count):
        part_copy(k).wait_recv()
        stat_copy(k).wait_recv()
        max_here = maxima[k, 0:rows]
        total_here = jnp.sum(totals[k, 0:rows], axis=1, keepdims=True)
        max_there = jnp.transpose(jnp.broadcast_to(stat_in[k, 0:1], (HD, rows)))
        total_there = jnp.transpose(jnp.broadcast_to(stat_in[k, 8:9], (HD, rows)))
        top = jnp.maximum(max_here, max_there)
        keep = jnp.exp2((max_here - top) * SCALE2)
        add = jnp.exp2((max_there - top) * SCALE2)
        total = total_here * keep + total_there * add
        value = summed[k, 0:rows] * keep + part_in[k].astype(F32) * add
        att[k] = (value / total).astype(BF16)
        cfg_copy(k).start()

    weight_copy.wait()
    mine = jnp.where(cfg == 0, GUIDE, 1.0 - GUIDE)
    theirs = jnp.where(cfg == 0, 1.0 - GUIDE, GUIDE)
    for k in range(count):
        cfg_copy(k).wait_recv()
        mixed[:, k * HD : (k + 1) * HD] = (
            mine * att[k].astype(F32) + theirs * att_other[k].astype(F32)
        ).astype(BF16)

    piece = 512 if half % 512 == 0 else half
    pieces = half // piece

    def rs_copy(i, j):
        columns = pl.ds(j * piece, piece)
        return remote(
            rs_out.at[lax.rem(head + i, nh), :, columns],
            rs_in.at[i, :, columns],
            rs_send.at[i, j],
            rs_recv.at[i, j],
            peers[i - 1],
        )

    for j in range(pieces):
        columns = pl.ds(j * piece, piece)
        result = jnp.dot(mixed[...], weight[:, columns], preferred_element_type=F32)
        rs_out[:, :, columns] = result.astype(BF16).reshape(nh, tok, piece)
        for i in range(1, nh):
            rs_copy(i, j).start()
    tokens_copy.wait()
    gate_copy.wait()
    for j in range(pieces):
        columns = pl.ds(j * piece, piece)
        for i in range(1, nh):
            rs_copy(i, j).wait_recv()
        value = rs_out[head, :, columns].astype(F32)
        for i in range(1, nh):
            value = value + rs_in[i, :, columns].astype(F32)
        scaled = gate[columns].reshape(1, piece) * value
        guided_ref[:, columns] = (tokens[:, columns].astype(F32) + scaled).astype(BF16)

    next_copy.wait()
    query_copy.wait_send()
    for n in range(last + count - WINDOW, last + count):
        for side in range(2):
            chunk(n, side).wait_send()
    for k in range(count):
        part_copy(k).wait_send()
        stat_copy(k).wait_send()
        cfg_copy(k).wait_send()

    for i in range(1, nh):
        a2a_to(i).wait_send()
        for j in range(pieces):
            rs_copy(i, j).wait_send()


def solution(mesh):
    nz = mesh.shape["patch"] // 2
    nh = mesh.shape["head"]

    def body(qkv, stale_kv, tokens_in, out_weight, gate):
        tok = qkv.shape[2]
        rows = tok * nh
        width = stale_kv.shape[3]
        count = width // HD
        half = tokens_in.shape[1]
        nfull = nz // 2 - 1
        pieces = half // 512 if half % 512 == 0 else 1
        anywhere = pl.BlockSpec(memory_space=pl.ANY)
        dma = pltpu.SemaphoreType.DMA
        return pl.pallas_call(
            functools.partial(kernel, nz, nh),
            out_shape=(
                jax.ShapeDtypeStruct((1, 2, rows, width), BF16),
                jax.ShapeDtypeStruct((tok, half), BF16),
            ),
            in_specs=[anywhere] * 5,
            out_specs=(anywhere, pl.BlockSpec(memory_space=pltpu.VMEM)),
            scratch_shapes=[
                pltpu.VMEM((3, rows, width), BF16),
                pltpu.VMEM((2, rows, width), BF16),
                pltpu.VMEM((nfull * count, 2, 2, rows, HD), BF16),
                pltpu.VMEM((count, 2, rows, HD), BF16),
                pltpu.VMEM((count, 2 * rows, HD), BF16),
                pltpu.VMEM((rows, width), BF16),
                pltpu.VMEM((count, 2 * rows, HD), F32),
                pltpu.VMEM((count, 2 * rows, HD), F32),
                pltpu.VMEM((count, 2 * rows, HD), F32),
                pltpu.VMEM((count, rows, HD), BF16),
                pltpu.VMEM((count, rows, HD), BF16),
                pltpu.VMEM((count, 16, rows), F32),
                pltpu.VMEM((count, 16, rows), F32),
                pltpu.VMEM((count, rows, HD), BF16),
                pltpu.VMEM((count, rows, HD), BF16),
                pltpu.VMEM((rows, width), BF16),
                pltpu.VMEM((width, half), BF16),
                pltpu.VMEM((tok, half), BF16),
                pltpu.VMEM((half,), F32),
                pltpu.VMEM((nh, tok, half), BF16),
                pltpu.VMEM((nh, tok, half), BF16),
                dma((2, (2 * nfull + 1) * count)),
                dma((2, (2 * nfull + 1) * count)),
                dma((nh,)),
                dma((nh,)),
                dma((2, count + 1)),
                dma((2, count + 1)),
                dma((count,)),
                dma((count,)),
                dma((nh, pieces)),
                dma((nh, pieces)),
                dma((6,)),
            ],
            compiler_params=pltpu.CompilerParams(
                collective_id=0, has_side_effects=True, vmem_limit_bytes=62 * 1024 * 1024
            ),
        )(qkv, stale_kv, tokens_in, out_weight, gate)

    in_specs = (
        P("cfg", None, ("patch", "head"), None),
        P("cfg", None, "patch", "head"),
        P(("patch", "head"), "cfg"),
        P("head", None),
        P("cfg"),
    )
    out_specs = (P("cfg", None, "patch", "head"), P(("patch", "head"), "cfg"))
    return jax.shard_map(body, mesh=mesh, in_specs=in_specs, out_specs=out_specs, check_vma=False)
```

```python
import functools
import math

import jax
import jax.numpy as jnp
from jax import lax
from jax.experimental import pallas as pl
from jax.experimental.pallas import tpu as pltpu
from jax.sharding import PartitionSpec as P

HD = 128
GUIDE = 6.0
MESH = pl.DeviceIdType.MESH
BF16 = jnp.bfloat16
F32 = jnp.float32
SCALE2 = HD ** (-0.5) * math.log2(math.e)


def kernel(
    nz,
    nh,
    qkv_ref,
    stale_ref,
    tokens_ref,
    weight_ref,
    gate_ref,
    next_ref,
    guided_ref,
    fresh,
    own,
    kv,
    far,
    qc,
    qpart,
    maxima,
    totals,
    summed,
    part_out,
    part_in,
    stat_out,
    stat_in,
    att,
    tiles,
    weight,
    tokens,
    gate,
    sums,
    rs_out,
    rs_in,
    ring_send,
    ring_recv,
    a2a_send,
    a2a_recv,
    part_send,
    part_recv,
    tile_send,
    tile_recv,
    weight_send,
    weight_recv,
    rs_send,
    rs_recv,
    local_sem,
):
    tok = qkv_ref.shape[2]
    rows = tok * nh
    width = stale_ref.shape[3]
    count = width // HD
    half = tokens_ref.shape[1]
    nx = nh // 2
    nfull = nz // 2 - 1
    patch = lax.axis_index("patch")
    head = lax.axis_index("head")
    cfg = lax.axis_index("cfg")
    column = patch // nz
    z = lax.rem(patch, nz)
    ahead = {"patch": column * nz + lax.rem(z + 1, nz)}
    behind = {"patch": column * nz + lax.rem(z + nz - 1, nz)}
    partner = {"patch": lax.rem(patch + nz, 2 * nz)}
    around = (ahead, behind)
    peers = [{"head": lax.rem(head + i, nh)} for i in range(1, nh)]
    x = lax.rem(head, nx)
    y_hi = head // nx
    opposite = {"head": (1 - y_hi) * nx + x}

    def x_peer(i):
        return {"head": y_hi * nx + lax.rem(x + i, nx)}

    def x_cross(i):
        return {"head": y_hi * nx + lax.rem(x + i, nx), "cfg": 1 - cfg}

    def remote(src, dst, send, recv, device):
        return pltpu.make_async_remote_copy(
            src_ref=src,
            dst_ref=dst,
            send_sem=send,
            recv_sem=recv,
            device_id=device,
            device_id_type=MESH,
        )

    block = 2 * count
    last = nfull * block

    def ring_own(n, side):
        k, part = n // 2, n % 2
        return remote(
            stale_ref.at[0, part, :, pl.ds(k * HD, HD)],
            kv.at[k, part, side],
            ring_send.at[side, n],
            ring_recv.at[side, n],
            around[side],
        )

    def ring_next(u, part, side):
        return remote(
            kv.at[u - count, part, side],
            kv.at[u, part, side],
            ring_send.at[side, 2 * u + part],
            ring_recv.at[side, 2 * u + part],
            around[side],
        )

    def ring_far(k, side):
        return remote(
            kv.at[(nfull - 1) * count + k, side, side],
            far.at[k, side],
            ring_send.at[side, last + k],
            ring_recv.at[side, last + k],
            around[side],
        )

    def chunk(n, side):
        return remote(
            far.at[0, side],
            far.at[0, side],
            ring_send.at[side, n],
            ring_recv.at[side, n],
            around[side],
        )

    def a2a_to(i):
        target = lax.rem(head + i, nh)
        return remote(
            qkv_ref.at[0, :, :, pl.ds(pl.multiple_of(target * width, HD), width)],
            fresh.at[:, pl.ds(pl.multiple_of(head * tok, tok), tok)],
            a2a_send.at[i],
            a2a_recv.at[i],
            peers[i - 1],
        )

    features = pl.ds(pl.multiple_of(cfg * half, HD), half)
    part_rows = width // 4

    def weight_to(i, j):
        span = pl.ds(j * part_rows, part_rows)
        return remote(
            weight_ref.at[span, features],
            weight.at[x, span],
            weight_send.at[i, j],
            weight_recv.at[i, j],
            x_peer(i),
        )

    own_copy = pltpu.make_async_copy(stale_ref.at[0], own, local_sem.at[0])
    mine_copy = pltpu.make_async_copy(
        qkv_ref.at[0, :, :, pl.ds(pl.multiple_of(head * width, HD), width)],
        fresh.at[:, pl.ds(pl.multiple_of(head * tok, tok), tok)],
        local_sem.at[1],
    )
    weight_copy = pltpu.make_async_copy(
        weight_ref.at[:, features], weight.at[x], local_sem.at[2]
    )
    tokens_copy = pltpu.make_async_copy(tokens_ref, tokens, local_sem.at[3])
    gate_copy = pltpu.make_async_copy(gate_ref, gate, local_sem.at[4])
    next_copy = pltpu.make_async_copy(fresh.at[pl.ds(1, 2)], next_ref.at[0], local_sem.at[5])

    barrier = pltpu.get_barrier_semaphore()
    greeted = [ahead, behind, partner] + peers + [x_cross(i) for i in range(nx)]
    for device in greeted:
        pl.semaphore_signal(barrier, inc=1, device_id=device, device_id_type=MESH)
    own_copy.start()
    mine_copy.start()
    weight_copy.start()
    tokens_copy.start()
    gate_copy.start()
    pl.semaphore_wait(barrier, len(greeted))

    for n in range(block):
        for side in range(2):
            ring_own(n, side).start()
        if n == block - 1:
            for i in range(1, nh):
                a2a_to(i).start()

    def pass_on(u):
        for part in range(2):
            n = 2 * u + part
            for side in range(2):
                chunk(n - block, side).wait_recv()
                ring_next(u, part, side).start()

    def attend(k, start, size, keys, values, first=False):
        span = pl.ds(start, size)
        scores = lax.dot_general(
            qc[k, span], keys, (((1,), (1,)), ((), ())), preferred_element_type=F32
        )
        block_max = jnp.max(scores, axis=1, keepdims=True)
        if first:
            new_max = jnp.broadcast_to(block_max, (size, HD))
        else:
            old_max = maxima[k, span]
            new_max = jnp.maximum(old_max, block_max)
            factor = jnp.exp2((old_max - new_max) * SCALE2)
        lanes = [
            jnp.exp2((scores[:, j : j + HD] - new_max) * SCALE2)
            for j in range(0, scores.shape[1], HD)
        ]
        total = functools.reduce(jnp.add, lanes)
        weights = jnp.concatenate([lane.astype(BF16) for lane in lanes], axis=1)
        product = jnp.dot(weights, values, preferred_element_type=F32)
        maxima[k, span] = new_max
        if first:
            totals[k, span] = total
            summed[k, span] = product
        else:
            totals[k, span] = totals[k, span] * factor + total
            summed[k, span] = summed[k, span] * factor + product

    def attend_chunk(v):
        k = lax.rem(v, count)
        keys = kv[v, 0].reshape(2 * rows, HD)
        values = kv[v, 1].reshape(2 * rows, HD)
        for start in (0, rows):
            attend(k, start, rows, keys, values)

    def loop(low, high, work):
        def step(i, carry):
            work(i)
            return carry

        lax.fori_loop(low, high, step, 0)

    chunks = nfull * count
    begin = min(3 * count, chunks)
    loop(count, min(2 * count, chunks), pass_on)
    mine_copy.wait()
    for i in range(1, nh):
        a2a_to(i).wait_recv()
    query_copy = remote(
        fresh.at[0], qpart, part_send.at[0, count], part_recv.at[0, count], partner
    )
    query_copy.start()
    next_copy.start()
    for j in range(4):
        for i in range(1, nx):
            weight_to(i, j).start()
    for k in range(count):
        qc[k, 0:rows] = fresh[0, :, k * HD : (k + 1) * HD]
    loop(min(2 * count, chunks), begin, pass_on)
    own_copy.wait()
    query_copy.wait_recv()
    for k in range(count):
        columns = slice(k * HD, (k + 1) * HD)
        qc[k, rows : 2 * rows] = qpart[:, columns]
        attend(k, 0, rows, fresh[1, :, columns], fresh[2, :, columns], first=True)
        attend(k, rows, rows, own[0, :, columns], own[1, :, columns], first=True)

    double = max(0, min(chunks - begin, begin - count))

    def catch_up(i):
        pass_on(begin + i)
        loop(2 * i, 2 * i + 2, attend_chunk)

    def follow(u):
        pass_on(u)
        attend_chunk(u - count)

    loop(0, double, catch_up)
    loop(begin + double, chunks, follow)
    done = 2 * double + max(0, chunks - begin - double)
    loop(done, chunks - count, attend_chunk)
    for k in range(count):
        u = chunks - count + k
        for side in range(2):
            for part in range(2):
                chunk(2 * u + part, side).wait_recv()
            ring_far(k, side).start()
        attend_chunk(u)

    def part_copy(k):
        return remote(
            part_out.at[k], part_in.at[k], part_send.at[0, k], part_recv.at[0, k], partner
        )

    def stat_copy(k):
        return remote(
            stat_out.at[k], stat_in.at[k], part_send.at[1, k], part_recv.at[1, k], partner
        )

    crossing = [(1, i) for i in range(nx)] + [(0, i) for i in range(1, nx)]

    def tile_copy(k, flip, i):
        return remote(
            att.at[k, :, lax.rem(x + i, nx)],
            tiles.at[k, cfg, x],
            tile_send.at[k, flip, i],
            tile_recv.at[k, flip, i],
            x_cross(i) if flip else x_peer(i),
        )

    lane = lax.broadcasted_iota(jnp.int32, (rows, HD), 1)
    for k in range(count):
        for side in range(2):
            chunk(last + k, side).wait_recv()
        attend(k, rows, rows, far[k, 0], far[k, 1])
        part_out[k] = summed[k, rows : 2 * rows].astype(BF16)
        part_copy(k).start()
        total = jnp.sum(totals[k, rows : 2 * rows], axis=1, keepdims=True)
        stats = jnp.where(lane < HD // 2, maxima[k, rows : 2 * rows], total)
        stat_out[k] = jnp.transpose(stats)[HD // 2 - 8 : HD // 2 + 8]
        stat_copy(k).start()
        attend(k, 0, rows, far[k, 0], far[k, 1])

    for k in range(count):
        stat_copy(k).wait_recv()
        max_here = maxima[k, 0:rows]
        total_here = jnp.sum(totals[k, 0:rows], axis=1, keepdims=True)
        max_there = jnp.transpose(jnp.broadcast_to(stat_in[k, 0:1], (HD, rows)))
        total_there = jnp.transpose(jnp.broadcast_to(stat_in[k, 8:9], (HD, rows)))
        top = jnp.maximum(max_here, max_there)
        keep = jnp.exp2((max_here - top) * SCALE2)
        add = jnp.exp2((max_there - top) * SCALE2)
        total = total_here * keep + total_there * add
        part_copy(k).wait_recv()
        value = summed[k, 0:rows] * keep + part_in[k].astype(F32) * add
        att[k] = (value / total).astype(BF16).reshape(2, nx, tok, HD)
        for flip, i in crossing:
            tile_copy(k, flip, i).start()
        tiles[k, cfg, x] = att[k, :, x]

    weight_copy.wait()
    for i in range(1, nx):
        for j in range(4):
            weight_to(i, j).wait_recv()
    tokens_copy.wait()
    gate_copy.wait()
    piece = 512 if half % 512 == 0 else half
    pieces = half // piece

    def rs_copy(j):
        columns = pl.ds(j * piece, piece)
        return remote(
            rs_out.at[:, columns], rs_in.at[:, columns], rs_send.at[j], rs_recv.at[j], opposite
        )

    for k in range(count):
        for flip, i in crossing:
            tile_copy(k, flip, i).wait_recv()
        both = GUIDE * tiles[k, 0].astype(F32) + (1.0 - GUIDE) * tiles[k, 1].astype(F32)
        both = both.astype(BF16)
        table = jnp.concatenate([both[i].reshape(2 * tok, HD) for i in range(nx)], axis=1)
        for j in range(pieces):
            columns = pl.ds(j * piece, piece)
            factors = weight[:, k * HD : (k + 1) * HD, columns].reshape(nx * HD, piece)
            result = jnp.dot(table, factors, preferred_element_type=F32)
            result = result.reshape(2, tok, piece)
            if k == 0:
                sums[:, :, columns] = result
            else:
                sums[:, :, columns] += result
            if k == count - 1:
                rs_out[:, columns] = sums[1 - y_hi, :, columns].astype(BF16)
                rs_copy(j).start()
    next_copy.wait()
    query_copy.wait_send()

    def sent(n):
        for side in range(2):
            chunk(n, side).wait_send()

    loop(0, last + count, sent)
    for k in range(count):
        part_copy(k).wait_send()
        stat_copy(k).wait_send()
        for flip, i in crossing:
            tile_copy(k, flip, i).wait_send()
    for i in range(1, nh):
        a2a_to(i).wait_send()
    for i in range(1, nx):
        for j in range(4):
            weight_to(i, j).wait_send()
    for j in range(pieces):
        columns = pl.ds(j * piece, piece)
        rs_copy(j).wait_recv()
        value = sums[y_hi, :, columns] + rs_in[:, columns].astype(F32)
        scaled = gate[columns].reshape(1, piece) * value
        guided_ref[:, columns] = (tokens[:, columns].astype(F32) + scaled).astype(BF16)
    for j in range(pieces):
        rs_copy(j).wait_send()


def solution(mesh):
    nz = mesh.shape["patch"] // 2
    nh = mesh.shape["head"]

    def body(qkv, stale_kv, tokens_in, out_weight, gate):
        tok = qkv.shape[2]
        rows = tok * nh
        width = stale_kv.shape[3]
        count = width // HD
        half = tokens_in.shape[1]
        nx = nh // 2
        nfull = nz // 2 - 1
        pieces = half // 512 if half % 512 == 0 else 1
        anywhere = pl.BlockSpec(memory_space=pl.ANY)
        dma = pltpu.SemaphoreType.DMA
        return pl.pallas_call(
            functools.partial(kernel, nz, nh),
            out_shape=(
                jax.ShapeDtypeStruct((1, 2, rows, width), BF16),
                jax.ShapeDtypeStruct((tok, half), BF16),
            ),
            in_specs=[anywhere] * 5,
            out_specs=(anywhere, pl.BlockSpec(memory_space=pltpu.VMEM)),
            scratch_shapes=[
                pltpu.VMEM((3, rows, width), BF16),
                pltpu.VMEM((2, rows, width), BF16),
                pltpu.VMEM((nfull * count, 2, 2, rows, HD), BF16),
                pltpu.VMEM((count, 2, rows, HD), BF16),
                pltpu.VMEM((count, 2 * rows, HD), BF16),
                pltpu.VMEM((rows, width), BF16),
                pltpu.VMEM((count, 2 * rows, HD), F32),
                pltpu.VMEM((count, 2 * rows, HD), F32),
                pltpu.VMEM((count, 2 * rows, HD), F32),
                pltpu.VMEM((count, rows, HD), BF16),
                pltpu.VMEM((count, rows, HD), BF16),
                pltpu.VMEM((count, 16, rows), F32),
                pltpu.VMEM((count, 16, rows), F32),
                pltpu.VMEM((count, 2, nx, tok, HD), BF16),
                pltpu.VMEM((count, 2, nx, 2, tok, HD), BF16),
                pltpu.VMEM((nx, width, half), BF16),
                pltpu.VMEM((tok, half), BF16),
                pltpu.VMEM((half,), F32),
                pltpu.VMEM((2, tok, half), F32),
                pltpu.VMEM((tok, half), BF16),
                pltpu.VMEM((tok, half), BF16),
                dma((2, (2 * nfull + 1) * count)),
                dma((2, (2 * nfull + 1) * count)),
                dma((nh,)),
                dma((nh,)),
                dma((2, count + 1)),
                dma((2, count + 1)),
                dma((count, 2, nx)),
                dma((count, 2, nx)),
                dma((nx, 4)),
                dma((nx, 4)),
                dma((pieces,)),
                dma((pieces,)),
                dma((6,)),
            ],
            compiler_params=pltpu.CompilerParams(
                collective_id=0, has_side_effects=True, vmem_limit_bytes=62 * 1024 * 1024
            ),
        )(qkv, stale_kv, tokens_in, out_weight, gate)

    in_specs = (
        P("cfg", None, ("patch", "head"), None),
        P("cfg", None, "patch", "head"),
        P(("patch", "head"), "cfg"),
        P("head", None),
        P("cfg"),
    )
    out_specs = (P("cfg", None, "patch", "head"), P(("patch", "head"), "cfg"))
    return jax.shard_map(body, mesh=mesh, in_specs=in_specs, out_specs=out_specs, check_vma=False)
```

```python
import functools
import math

import jax
import jax.numpy as jnp
from jax import lax
from jax.experimental import pallas as pl
from jax.experimental.pallas import tpu as pltpu
from jax.sharding import PartitionSpec as P

HD = 128
GUIDE = 6.0
MESH = pl.DeviceIdType.MESH
BF16 = jnp.bfloat16
F32 = jnp.float32
SCALE2 = HD ** (-0.5) * math.log2(math.e)


def kernel(
    nz,
    nh,
    qkv_ref,
    stale_ref,
    tokens_ref,
    weight_ref,
    gate_ref,
    next_ref,
    guided_ref,
    fresh,
    own,
    kv,
    far,
    qc,
    qpart,
    maxima,
    totals,
    summed,
    part_out,
    part_in,
    stat_out,
    stat_in,
    att,
    tiles,
    weight,
    tokens,
    gate,
    sums,
    rs_out,
    rs_in,
    ring_send,
    ring_recv,
    a2a_send,
    a2a_recv,
    part_send,
    part_recv,
    tile_send,
    tile_recv,
    weight_send,
    weight_recv,
    rs_send,
    rs_recv,
    local_sem,
):
    tok = qkv_ref.shape[2]
    rows = tok * nh
    width = stale_ref.shape[3]
    count = width // HD
    half = tokens_ref.shape[1]
    nx = nh // 2
    nfull = nz // 2 - 1
    patch = lax.axis_index("patch")
    head = lax.axis_index("head")
    cfg = lax.axis_index("cfg")
    column = patch // nz
    z = lax.rem(patch, nz)
    ahead = {"patch": column * nz + lax.rem(z + 1, nz)}
    behind = {"patch": column * nz + lax.rem(z + nz - 1, nz)}
    partner = {"patch": lax.rem(patch + nz, 2 * nz)}
    around = (ahead, behind)
    peers = [{"head": lax.rem(head + i, nh)} for i in range(1, nh)]
    x = lax.rem(head, nx)
    y_hi = head // nx
    opposite = {"head": (1 - y_hi) * nx + x}

    def x_peer(i):
        return {"head": y_hi * nx + lax.rem(x + i, nx)}

    def x_cross(i):
        return {"head": y_hi * nx + lax.rem(x + i, nx), "cfg": 1 - cfg}

    def remote(src, dst, send, recv, device):
        return pltpu.make_async_remote_copy(
            src_ref=src,
            dst_ref=dst,
            send_sem=send,
            recv_sem=recv,
            device_id=device,
            device_id_type=MESH,
        )

    last = nfull * count

    def ring(src, dst, n, side):
        return remote(src, dst, ring_send.at[side, n], ring_recv.at[side, n], around[side])

    def ring_own(k, side):
        return ring(
            stale_ref.at[0, :, :, pl.ds(k * HD, HD)], kv.at[k, :, side], k, side
        )

    def ring_next(u, side):
        return ring(kv.at[u - count, :, side], kv.at[u, :, side], u, side)

    def ring_far(k, side):
        return ring(kv.at[last - count + k, side, side], far.at[k, side], last + k, side)

    def chunk(n, side):
        return ring(kv.at[0, :, side], kv.at[0, :, side], n, side)

    def a2a_to(i):
        target = lax.rem(head + i, nh)
        return remote(
            qkv_ref.at[0, :, :, pl.ds(pl.multiple_of(target * width, HD), width)],
            fresh.at[:, pl.ds(pl.multiple_of(head * tok, tok), tok)],
            a2a_send.at[i],
            a2a_recv.at[i],
            peers[i - 1],
        )

    features = pl.ds(pl.multiple_of(cfg * half, HD), half)
    part_rows = width // 4

    def weight_to(i, j):
        span = pl.ds(j * part_rows, part_rows)
        return remote(
            weight_ref.at[span, features],
            weight.at[x, span],
            weight_send.at[i, j],
            weight_recv.at[i, j],
            x_peer(i),
        )

    own_copy = pltpu.make_async_copy(stale_ref.at[0], own, local_sem.at[0])
    mine_copy = pltpu.make_async_copy(
        qkv_ref.at[0, :, :, pl.ds(pl.multiple_of(head * width, HD), width)],
        fresh.at[:, pl.ds(pl.multiple_of(head * tok, tok), tok)],
        local_sem.at[1],
    )
    weight_copy = pltpu.make_async_copy(
        weight_ref.at[:, features], weight.at[x], local_sem.at[2]
    )
    tokens_copy = pltpu.make_async_copy(tokens_ref, tokens, local_sem.at[3])
    gate_copy = pltpu.make_async_copy(gate_ref, gate, local_sem.at[4])
    next_copy = pltpu.make_async_copy(fresh.at[pl.ds(1, 2)], next_ref.at[0], local_sem.at[5])

    barrier = pltpu.get_barrier_semaphore()
    greeted = [ahead, behind, partner] + peers + [x_cross(i) for i in range(nx)]
    for device in greeted:
        pl.semaphore_signal(barrier, inc=1, device_id=device, device_id_type=MESH)
    own_copy.start()
    mine_copy.start()
    weight_copy.start()
    tokens_copy.start()
    gate_copy.start()
    pl.semaphore_wait(barrier, len(greeted))

    for k in range(count):
        for side in range(2):
            ring_own(k, side).start()
    for i in range(1, nh):
        a2a_to(i).start()

    def pass_on(u):
        for side in range(2):
            chunk(u - count, side).wait_recv()
            ring_next(u, side).start()

    def attend(k, start, size, keys, values, first=False):
        span = pl.ds(start, size)
        scores = lax.dot_general(
            qc[k, span], keys, (((1,), (1,)), ((), ())), preferred_element_type=F32
        )
        block_max = jnp.max(scores, axis=1, keepdims=True)
        if first:
            new_max = jnp.broadcast_to(block_max, (size, HD))
        else:
            old_max = maxima[k, span]
            new_max = jnp.maximum(old_max, block_max)
            factor = jnp.exp2((old_max - new_max) * SCALE2)
        lanes = [
            jnp.exp2((scores[:, j : j + HD] - new_max) * SCALE2)
            for j in range(0, scores.shape[1], HD)
        ]
        total = functools.reduce(jnp.add, lanes)
        weights = jnp.concatenate([lane.astype(BF16) for lane in lanes], axis=1)
        product = jnp.dot(weights, values, preferred_element_type=F32)
        maxima[k, span] = new_max
        if first:
            totals[k, span] = total
            summed[k, span] = product
        else:
            totals[k, span] = totals[k, span] * factor + total
            summed[k, span] = summed[k, span] * factor + product

    def attend_chunk(v):
        k = lax.rem(v, count)
        keys = kv[v, 0].reshape(2 * rows, HD)
        values = kv[v, 1].reshape(2 * rows, HD)
        for start in (0, rows):
            attend(k, start, rows, keys, values)

    def loop(low, high, work):
        def step(i, carry):
            work(i)
            return carry

        lax.fori_loop(low, high, step, 0)

    chunks = nfull * count
    begin = min(3 * count, chunks)
    loop(count, min(2 * count, chunks), pass_on)
    mine_copy.wait()
    for i in range(1, nh):
        a2a_to(i).wait_recv()
    query_copy = remote(
        fresh.at[0], qpart, part_send.at[0, count], part_recv.at[0, count], partner
    )
    query_copy.start()
    next_copy.start()
    for j in range(4):
        for i in range(1, nx):
            weight_to(i, j).start()
    for k in range(count):
        qc[k, 0:rows] = fresh[0, :, k * HD : (k + 1) * HD]
    loop(min(2 * count, chunks), begin, pass_on)
    own_copy.wait()
    query_copy.wait_recv()
    for k in range(count):
        columns = slice(k * HD, (k + 1) * HD)
        qc[k, rows : 2 * rows] = qpart[:, columns]
        attend(k, 0, rows, fresh[1, :, columns], fresh[2, :, columns], first=True)
        attend(k, rows, rows, own[0, :, columns], own[1, :, columns], first=True)

    double = max(0, min(chunks - begin, begin - count))

    def catch_up(i):
        pass_on(begin + i)
        loop(2 * i, 2 * i + 2, attend_chunk)

    def follow(u):
        pass_on(u)
        attend_chunk(u - count)

    loop(0, double, catch_up)
    loop(begin + double, chunks, follow)
    done = 2 * double + max(0, chunks - begin - double)
    loop(done, chunks - count, attend_chunk)
    for k in range(count):
        u = chunks - count + k
        for side in range(2):
            chunk(u, side).wait_recv()
            ring_far(k, side).start()
        attend_chunk(u)

    def part_copy(k):
        return remote(
            part_out.at[k], part_in.at[k], part_send.at[0, k], part_recv.at[0, k], partner
        )

    def stat_copy(k):
        return remote(
            stat_out.at[k], stat_in.at[k], part_send.at[1, k], part_recv.at[1, k], partner
        )

    crossing = [(1, i) for i in range(nx)] + [(0, i) for i in range(1, nx)]

    def tile_copy(k, flip, i):
        return remote(
            att.at[k, :, lax.rem(x + i, nx)],
            tiles.at[k, cfg, x],
            tile_send.at[k, flip, i],
            tile_recv.at[k, flip, i],
            x_cross(i) if flip else x_peer(i),
        )

    lane = lax.broadcasted_iota(jnp.int32, (rows, HD), 1)
    for k in range(count):
        for side in range(2):
            ring_far(k, side).wait_recv()
        attend(k, rows, rows, far[k, 0], far[k, 1])
        part_out[k] = summed[k, rows : 2 * rows].astype(BF16)
        part_copy(k).start()
        total = jnp.sum(totals[k, rows : 2 * rows], axis=1, keepdims=True)
        stats = jnp.where(lane < HD // 2, maxima[k, rows : 2 * rows], total)
        stat_out[k] = jnp.transpose(stats)[HD // 2 - 8 : HD // 2 + 8]
        stat_copy(k).start()
        attend(k, 0, rows, far[k, 0], far[k, 1])

    for k in range(count):
        stat_copy(k).wait_recv()
        max_here = maxima[k, 0:rows]
        total_here = jnp.sum(totals[k, 0:rows], axis=1, keepdims=True)
        max_there = jnp.transpose(jnp.broadcast_to(stat_in[k, 0:1], (HD, rows)))
        total_there = jnp.transpose(jnp.broadcast_to(stat_in[k, 8:9], (HD, rows)))
        top = jnp.maximum(max_here, max_there)
        keep = jnp.exp2((max_here - top) * SCALE2)
        add = jnp.exp2((max_there - top) * SCALE2)
        total = total_here * keep + total_there * add
        part_copy(k).wait_recv()
        value = summed[k, 0:rows] * keep + part_in[k].astype(F32) * add
        att[k] = (value / total).astype(BF16).reshape(2, nx, tok, HD)
        for flip, i in crossing:
            tile_copy(k, flip, i).start()
        tiles[k, cfg, x] = att[k, :, x]

    weight_copy.wait()
    for i in range(1, nx):
        for j in range(4):
            weight_to(i, j).wait_recv()
    tokens_copy.wait()
    gate_copy.wait()
    piece = 512 if half % 512 == 0 else half
    pieces = half // piece

    def rs_copy(j):
        columns = pl.ds(j * piece, piece)
        return remote(
            rs_out.at[:, columns], rs_in.at[:, columns], rs_send.at[j], rs_recv.at[j], opposite
        )

    for k in range(count):
        for flip, i in crossing:
            tile_copy(k, flip, i).wait_recv()
        both = GUIDE * tiles[k, 0].astype(F32) + (1.0 - GUIDE) * tiles[k, 1].astype(F32)
        both = both.astype(BF16)
        table = jnp.concatenate([both[i].reshape(2 * tok, HD) for i in range(nx)], axis=1)
        for j in range(pieces):
            columns = pl.ds(j * piece, piece)
            factors = weight[:, k * HD : (k + 1) * HD, columns].reshape(nx * HD, piece)
            result = jnp.dot(table, factors, preferred_element_type=F32)
            result = result.reshape(2, tok, piece)
            if k == 0:
                sums[:, :, columns] = result
            else:
                sums[:, :, columns] += result
            if k == count - 1:
                rs_out[:, columns] = sums[1 - y_hi, :, columns].astype(BF16)
                rs_copy(j).start()
    next_copy.wait()
    query_copy.wait_send()

    def sent(n):
        for side in range(2):
            chunk(n, side).wait_send()

    loop(0, last, sent)
    for k in range(count):
        for side in range(2):
            ring_far(k, side).wait_send()
        part_copy(k).wait_send()
        stat_copy(k).wait_send()
        for flip, i in crossing:
            tile_copy(k, flip, i).wait_send()
    for i in range(1, nh):
        a2a_to(i).wait_send()
    for i in range(1, nx):
        for j in range(4):
            weight_to(i, j).wait_send()
    for j in range(pieces):
        columns = pl.ds(j * piece, piece)
        rs_copy(j).wait_recv()
        value = sums[y_hi, :, columns] + rs_in[:, columns].astype(F32)
        scaled = gate[columns].reshape(1, piece) * value
        guided_ref[:, columns] = (tokens[:, columns].astype(F32) + scaled).astype(BF16)
    for j in range(pieces):
        rs_copy(j).wait_send()


def solution(mesh):
    nz = mesh.shape["patch"] // 2
    nh = mesh.shape["head"]

    def body(qkv, stale_kv, tokens_in, out_weight, gate):
        tok = qkv.shape[2]
        rows = tok * nh
        width = stale_kv.shape[3]
        count = width // HD
        half = tokens_in.shape[1]
        nx = nh // 2
        nfull = nz // 2 - 1
        pieces = half // 512 if half % 512 == 0 else 1
        anywhere = pl.BlockSpec(memory_space=pl.ANY)
        dma = pltpu.SemaphoreType.DMA
        return pl.pallas_call(
            functools.partial(kernel, nz, nh),
            out_shape=(
                pltpu.VMEM((1, 2, rows, width), BF16),
                pltpu.VMEM((tok, half), BF16),
            ),
            in_specs=[anywhere] * 5,
            out_specs=(pl.BlockSpec(memory_space=pltpu.VMEM),) * 2,
            scratch_shapes=[
                pltpu.VMEM((3, rows, width), BF16),
                pltpu.VMEM((2, rows, width), BF16),
                pltpu.VMEM((nfull * count, 2, 2, rows, HD), BF16),
                pltpu.VMEM((count, 2, rows, HD), BF16),
                pltpu.VMEM((count, 2 * rows, HD), BF16),
                pltpu.VMEM((rows, width), BF16),
                pltpu.VMEM((count, 2 * rows, HD), F32),
                pltpu.VMEM((count, 2 * rows, HD), F32),
                pltpu.VMEM((count, 2 * rows, HD), F32),
                pltpu.VMEM((count, rows, HD), BF16),
                pltpu.VMEM((count, rows, HD), BF16),
                pltpu.VMEM((count, 16, rows), F32),
                pltpu.VMEM((count, 16, rows), F32),
                pltpu.VMEM((count, 2, nx, tok, HD), BF16),
                pltpu.VMEM((count, 2, nx, 2, tok, HD), BF16),
                pltpu.VMEM((nx, width, half), BF16),
                pltpu.VMEM((tok, half), BF16),
                pltpu.VMEM((half,), F32),
                pltpu.VMEM((2, tok, half), F32),
                pltpu.VMEM((tok, half), BF16),
                pltpu.VMEM((tok, half), BF16),
                dma((2, (nfull + 1) * count)),
                dma((2, (nfull + 1) * count)),
                dma((nh,)),
                dma((nh,)),
                dma((2, count + 1)),
                dma((2, count + 1)),
                dma((count, 2, nx)),
                dma((count, 2, nx)),
                dma((nx, 4)),
                dma((nx, 4)),
                dma((pieces,)),
                dma((pieces,)),
                dma((6,)),
            ],
            compiler_params=pltpu.CompilerParams(
                collective_id=0, has_side_effects=True, vmem_limit_bytes=62 * 1024 * 1024
            ),
        )(qkv, stale_kv, tokens_in, out_weight, gate)

    in_specs = (
        P("cfg", None, ("patch", "head"), None),
        P("cfg", None, "patch", "head"),
        P(("patch", "head"), "cfg"),
        P("head", None),
        P("cfg"),
    )
    out_specs = (P("cfg", None, "patch", "head"), P(("patch", "head"), "cfg"))
    return jax.shard_map(body, mesh=mesh, in_specs=in_specs, out_specs=out_specs, check_vma=False)
```

```python
import functools
import math

import jax
import jax.numpy as jnp
from jax import lax
from jax.experimental import pallas as pl
from jax.experimental.pallas import tpu as pltpu
from jax.sharding import PartitionSpec as P

HD = 128
GUIDE = 6.0
MESH = pl.DeviceIdType.MESH
BF16 = jnp.bfloat16
F32 = jnp.float32
SCALE2 = HD ** (-0.5) * math.log2(math.e)


def kernel(
    nz,
    nh,
    qkv_ref,
    stale_ref,
    tokens_ref,
    weight_ref,
    gate_ref,
    next_ref,
    guided_ref,
    fresh,
    own,
    kv,
    far,
    qc,
    qpart,
    maxima,
    totals,
    summed,
    part_out,
    part_in,
    stat_out,
    stat_in,
    att,
    tiles,
    weight,
    tokens,
    gate,
    sums,
    rs_out,
    rs_in,
    ring_send,
    ring_recv,
    a2a_send,
    a2a_recv,
    part_send,
    part_recv,
    tile_send,
    tile_recv,
    weight_send,
    weight_recv,
    rs_send,
    rs_recv,
    local_sem,
):
    tok = qkv_ref.shape[2]
    rows = tok * nh
    width = stale_ref.shape[3]
    count = width // HD
    half = tokens_ref.shape[1]
    nx = nh // 2
    nfull = nz // 2 - 1
    patch = lax.axis_index("patch")
    head = lax.axis_index("head")
    cfg = lax.axis_index("cfg")
    column = patch // nz
    z = lax.rem(patch, nz)
    ahead = {"patch": column * nz + lax.rem(z + 1, nz)}
    behind = {"patch": column * nz + lax.rem(z + nz - 1, nz)}
    partner = {"patch": lax.rem(patch + nz, 2 * nz)}
    around = (ahead, behind)
    peers = [{"head": lax.rem(head + i, nh)} for i in range(1, nh)]
    x = lax.rem(head, nx)
    y_hi = head // nx
    opposite = {"head": (1 - y_hi) * nx + x}

    def x_peer(i):
        return {"head": y_hi * nx + lax.rem(x + i, nx)}

    def x_cross(i):
        return {"head": y_hi * nx + lax.rem(x + i, nx), "cfg": 1 - cfg}

    def remote(src, dst, send, recv, device):
        return pltpu.make_async_remote_copy(
            src_ref=src,
            dst_ref=dst,
            send_sem=send,
            recv_sem=recv,
            device_id=device,
            device_id_type=MESH,
        )

    last = nfull * count

    def ring(src, dst, n, side):
        return remote(src, dst, ring_send.at[side, n], ring_recv.at[side, n], around[side])

    def ring_own(k, side):
        return ring(
            stale_ref.at[0, :, :, pl.ds(k * HD, HD)], kv.at[k, :, side], k, side
        )

    def ring_next(u, side):
        return ring(kv.at[u - count, :, side], kv.at[u, :, side], u, side)

    def ring_far(k, side):
        return ring(kv.at[last - count + k, side, side], far.at[k, side], last + k, side)

    def chunk(n, side):
        return ring(kv.at[0, :, side], kv.at[0, :, side], n, side)

    def a2a_to(i):
        target = lax.rem(head + i, nh)
        return remote(
            qkv_ref.at[0, :, :, pl.ds(pl.multiple_of(target * width, HD), width)],
            fresh.at[:, pl.ds(pl.multiple_of(head * tok, tok), tok)],
            a2a_send.at[i],
            a2a_recv.at[i],
            peers[i - 1],
        )

    features = pl.ds(pl.multiple_of(cfg * half, HD), half)
    part_rows = width // 4

    def weight_to(i, j):
        span = pl.ds(j * part_rows, part_rows)
        return remote(
            weight_ref.at[span, features],
            weight.at[x, span],
            weight_send.at[i, j],
            weight_recv.at[i, j],
            x_peer(i),
        )

    own_copy = pltpu.make_async_copy(stale_ref.at[0], own, local_sem.at[0])
    mine_copy = pltpu.make_async_copy(
        qkv_ref.at[0, :, :, pl.ds(pl.multiple_of(head * width, HD), width)],
        fresh.at[:, pl.ds(pl.multiple_of(head * tok, tok), tok)],
        local_sem.at[1],
    )
    weight_copy = pltpu.make_async_copy(
        weight_ref.at[:, features], weight.at[x], local_sem.at[2]
    )
    tokens_copy = pltpu.make_async_copy(tokens_ref, tokens, local_sem.at[3])
    gate_copy = pltpu.make_async_copy(gate_ref, gate, local_sem.at[4])
    next_copy = pltpu.make_async_copy(fresh.at[pl.ds(1, 2)], next_ref.at[0], local_sem.at[5])

    barrier = pltpu.get_barrier_semaphore()
    greeted = [ahead, behind, partner] + peers + [x_cross(i) for i in range(nx)]
    for device in greeted:
        pl.semaphore_signal(barrier, inc=1, device_id=device, device_id_type=MESH)
    own_copy.start()
    mine_copy.start()
    weight_copy.start()
    tokens_copy.start()
    gate_copy.start()
    pl.semaphore_wait(barrier, len(greeted))

    for k in range(count):
        for side in range(2):
            ring_own(k, side).start()
    for i in range(1, nh):
        a2a_to(i).start()

    def pass_on(u):
        for side in range(2):
            chunk(u - count, side).wait_recv()
            ring_next(u, side).start()

    def attend(k, start, size, keys, values, first=False):
        span = pl.ds(start, size)
        scores = lax.dot_general(
            qc[k, span], keys, (((1,), (1,)), ((), ())), preferred_element_type=F32
        )
        block_max = jnp.max(scores, axis=1, keepdims=True)
        if first:
            new_max = jnp.broadcast_to(block_max, (size, HD))
        else:
            old_max = maxima[k, span]
            new_max = jnp.maximum(old_max, block_max)
            factor = jnp.exp2((old_max - new_max) * SCALE2)
        lanes = [
            jnp.exp2((scores[:, j : j + HD] - new_max) * SCALE2)
            for j in range(0, scores.shape[1], HD)
        ]
        total = functools.reduce(jnp.add, lanes)
        weights = jnp.concatenate([lane.astype(BF16) for lane in lanes], axis=1)
        product = jnp.dot(weights, values, preferred_element_type=F32)
        maxima[k, span] = new_max
        if first:
            totals[k, span] = total
            summed[k, span] = product
        else:
            totals[k, span] = totals[k, span] * factor + total
            summed[k, span] = summed[k, span] * factor + product

    def attend_chunk(v):
        k = lax.rem(v, count)
        keys = kv[v, 0].reshape(2 * rows, HD)
        values = kv[v, 1].reshape(2 * rows, HD)
        for start in (0, rows):
            attend(k, start, rows, keys, values)

    def loop(low, high, work):
        def step(i, carry):
            work(i)
            return carry

        lax.fori_loop(low, high, step, 0)

    chunks = nfull * count
    begin = min(3 * count, chunks)
    loop(count, min(2 * count, chunks), pass_on)
    mine_copy.wait()
    for i in range(1, nh):
        a2a_to(i).wait_recv()
    query_copy = remote(
        fresh.at[0], qpart, part_send.at[0, count], part_recv.at[0, count], partner
    )
    query_copy.start()
    next_copy.start()
    for j in range(4):
        for i in range(1, nx):
            weight_to(i, j).start()
    for k in range(count):
        qc[k, 0:rows] = fresh[0, :, k * HD : (k + 1) * HD]
    loop(min(2 * count, chunks), begin, pass_on)
    own_copy.wait()
    query_copy.wait_recv()
    for k in range(count):
        columns = slice(k * HD, (k + 1) * HD)
        qc[k, rows : 2 * rows] = qpart[:, columns]
        attend(k, 0, rows, fresh[1, :, columns], fresh[2, :, columns], first=True)
        attend(k, rows, rows, own[0, :, columns], own[1, :, columns], first=True)

    double = max(0, min(chunks - begin, begin - count))

    def catch_up(i):
        pass_on(begin + i)
        loop(2 * i, 2 * i + 2, attend_chunk)

    def follow(u):
        pass_on(u)
        attend_chunk(u - count)

    loop(0, double, catch_up)
    loop(begin + double, chunks, follow)
    done = 2 * double + max(0, chunks - begin - double)
    loop(done, chunks - count, attend_chunk)
    for k in range(count):
        u = chunks - count + k
        for side in range(2):
            chunk(u, side).wait_recv()
            ring_far(k, side).start()
        attend_chunk(u)

    def part_copy(k):
        return remote(
            part_out.at[k], part_in.at[k], part_send.at[0, k], part_recv.at[0, k], partner
        )

    def stat_copy(k):
        return remote(
            stat_out.at[k], stat_in.at[k], part_send.at[1, k], part_recv.at[1, k], partner
        )

    crossing = [(1, i) for i in range(nx)] + [(0, i) for i in range(1, nx)]

    def tile_copy(k, flip, i):
        return remote(
            att.at[k, :, lax.rem(x + i, nx)],
            tiles.at[k, cfg, x],
            tile_send.at[k, flip, i],
            tile_recv.at[k, flip, i],
            x_cross(i) if flip else x_peer(i),
        )

    lane = lax.broadcasted_iota(jnp.int32, (rows, HD), 1)
    for k in range(count):
        for side in range(2):
            ring_far(k, side).wait_recv()
        attend(k, rows, rows, far[k, 0], far[k, 1])
        total = jnp.sum(totals[k, rows : 2 * rows], axis=1, keepdims=True)
        stats = jnp.where(lane < 4, maxima[k, rows : 2 * rows], total)
        stat_out[k] = jnp.transpose(stats)[0:8]
        stat_copy(k).start()
        part_out[k] = summed[k, rows : 2 * rows].astype(BF16)
        part_copy(k).start()
        attend(k, 0, rows, far[k, 0], far[k, 1])

    for k in range(count):
        max_here = maxima[k, 0:rows]
        total_here = jnp.sum(totals[k, 0:rows], axis=1, keepdims=True)
        stat_copy(k).wait_recv()
        max_there = jnp.transpose(jnp.broadcast_to(stat_in[k, 0:1], (HD, rows)))
        total_there = jnp.transpose(jnp.broadcast_to(stat_in[k, 4:5], (HD, rows)))
        top = jnp.maximum(max_here, max_there)
        keep = jnp.exp2((max_here - top) * SCALE2)
        add = jnp.exp2((max_there - top) * SCALE2)
        total = total_here * keep + total_there * add
        part_copy(k).wait_recv()
        value = summed[k, 0:rows] * keep + part_in[k].astype(F32) * add
        att[k] = (value / total).astype(BF16).reshape(2, nx, tok, HD)
        for flip, i in crossing:
            tile_copy(k, flip, i).start()
        tiles[k, cfg, x] = att[k, :, x]

    weight_copy.wait()
    for i in range(1, nx):
        for j in range(4):
            weight_to(i, j).wait_recv()
    tokens_copy.wait()
    gate_copy.wait()
    piece = 512 if half % 512 == 0 else half
    pieces = half // piece

    def rs_copy(j):
        columns = pl.ds(j * piece, piece)
        return remote(
            rs_out.at[:, columns], rs_in.at[:, columns], rs_send.at[j], rs_recv.at[j], opposite
        )

    for k in range(count):
        for flip, i in crossing:
            tile_copy(k, flip, i).wait_recv()
        both = GUIDE * tiles[k, 0].astype(F32) + (1.0 - GUIDE) * tiles[k, 1].astype(F32)
        both = both.astype(BF16)
        table = jnp.concatenate([both[i].reshape(2 * tok, HD) for i in range(nx)], axis=1)
        for j in range(pieces):
            columns = pl.ds(j * piece, piece)
            factors = weight[:, k * HD : (k + 1) * HD, columns].reshape(nx * HD, piece)
            result = jnp.dot(table, factors, preferred_element_type=F32)
            result = result.reshape(2, tok, piece)
            if k == 0:
                sums[:, :, columns] = result
            else:
                sums[:, :, columns] += result
            if k == count - 1:
                rs_out[:, columns] = sums[1 - y_hi, :, columns].astype(BF16)
                rs_copy(j).start()
    next_copy.wait()
    query_copy.wait_send()

    def sent(n):
        for side in range(2):
            chunk(n, side).wait_send()

    loop(0, last, sent)
    for k in range(count):
        for side in range(2):
            ring_far(k, side).wait_send()
        part_copy(k).wait_send()
        stat_copy(k).wait_send()
        for flip, i in crossing:
            tile_copy(k, flip, i).wait_send()
    for i in range(1, nh):
        a2a_to(i).wait_send()
    for i in range(1, nx):
        for j in range(4):
            weight_to(i, j).wait_send()
    for j in range(pieces):
        columns = pl.ds(j * piece, piece)
        rs_copy(j).wait_recv()
        value = sums[y_hi, :, columns] + rs_in[:, columns].astype(F32)
        scaled = gate[columns].reshape(1, piece) * value
        guided_ref[:, columns] = (tokens[:, columns].astype(F32) + scaled).astype(BF16)
    for j in range(pieces):
        rs_copy(j).wait_send()


def solution(mesh):
    nz = mesh.shape["patch"] // 2
    nh = mesh.shape["head"]

    def body(qkv, stale_kv, tokens_in, out_weight, gate):
        tok = qkv.shape[2]
        rows = tok * nh
        width = stale_kv.shape[3]
        count = width // HD
        half = tokens_in.shape[1]
        nx = nh // 2
        nfull = nz // 2 - 1
        pieces = half // 512 if half % 512 == 0 else 1
        anywhere = pl.BlockSpec(memory_space=pl.ANY)
        dma = pltpu.SemaphoreType.DMA
        return pl.pallas_call(
            functools.partial(kernel, nz, nh),
            out_shape=(
                pltpu.VMEM((1, 2, rows, width), BF16),
                pltpu.VMEM((tok, half), BF16),
            ),
            in_specs=[anywhere] * 5,
            out_specs=(pl.BlockSpec(memory_space=pltpu.VMEM),) * 2,
            scratch_shapes=[
                pltpu.VMEM((3, rows, width), BF16),
                pltpu.VMEM((2, rows, width), BF16),
                pltpu.VMEM((nfull * count, 2, 2, rows, HD), BF16),
                pltpu.VMEM((count, 2, rows, HD), BF16),
                pltpu.VMEM((count, 2 * rows, HD), BF16),
                pltpu.VMEM((rows, width), BF16),
                pltpu.VMEM((count, 2 * rows, HD), F32),
                pltpu.VMEM((count, 2 * rows, HD), F32),
                pltpu.VMEM((count, 2 * rows, HD), F32),
                pltpu.VMEM((count, rows, HD), BF16),
                pltpu.VMEM((count, rows, HD), BF16),
                pltpu.VMEM((count, 8, rows), F32),
                pltpu.VMEM((count, 8, rows), F32),
                pltpu.VMEM((count, 2, nx, tok, HD), BF16),
                pltpu.VMEM((count, 2, nx, 2, tok, HD), BF16),
                pltpu.VMEM((nx, width, half), BF16),
                pltpu.VMEM((tok, half), BF16),
                pltpu.VMEM((half,), F32),
                pltpu.VMEM((2, tok, half), F32),
                pltpu.VMEM((tok, half), BF16),
                pltpu.VMEM((tok, half), BF16),
                dma((2, (nfull + 1) * count)),
                dma((2, (nfull + 1) * count)),
                dma((nh,)),
                dma((nh,)),
                dma((2, count + 1)),
                dma((2, count + 1)),
                dma((count, 2, nx)),
                dma((count, 2, nx)),
                dma((nx, 4)),
                dma((nx, 4)),
                dma((pieces,)),
                dma((pieces,)),
                dma((6,)),
            ],
            compiler_params=pltpu.CompilerParams(
                collective_id=0, has_side_effects=True, vmem_limit_bytes=62 * 1024 * 1024
            ),
        )(qkv, stale_kv, tokens_in, out_weight, gate)

    in_specs = (
        P("cfg", None, ("patch", "head"), None),
        P("cfg", None, "patch", "head"),
        P(("patch", "head"), "cfg"),
        P("head", None),
        P("cfg"),
    )
    out_specs = (P("cfg", None, "patch", "head"), P(("patch", "head"), "cfg"))
    return jax.shard_map(body, mesh=mesh, in_specs=in_specs, out_specs=out_specs, check_vma=False)
```

```python
import functools
import math

import jax
import jax.numpy as jnp
from jax import lax
from jax.experimental import pallas as pl
from jax.experimental.pallas import tpu as pltpu
from jax.sharding import PartitionSpec as P

HD = 128
GUIDE = 6.0
MESH = pl.DeviceIdType.MESH
BF16 = jnp.bfloat16
F32 = jnp.float32
SCALE2 = HD ** (-0.5) * math.log2(math.e)


def kernel(
    nz,
    nh,
    qkv_ref,
    stale_ref,
    tokens_ref,
    weight_ref,
    gate_ref,
    next_ref,
    guided_ref,
    fresh,
    own,
    kv,
    far,
    qc,
    qpart,
    maxima,
    totals,
    summed,
    part_out,
    part_in,
    stat_out,
    stat_in,
    att,
    tiles,
    weight,
    tokens,
    gate,
    sums,
    rs_out,
    rs_in,
    ring_send,
    ring_recv,
    a2a_send,
    a2a_recv,
    part_send,
    part_recv,
    tile_send,
    tile_recv,
    weight_send,
    weight_recv,
    rs_send,
    rs_recv,
    local_sem,
):
    tok = qkv_ref.shape[2]
    rows = tok * nh
    width = stale_ref.shape[3]
    count = width // HD
    half = tokens_ref.shape[1]
    nx = nh // 2
    nfull = nz // 2 - 1
    patch = lax.axis_index("patch")
    head = lax.axis_index("head")
    cfg = lax.axis_index("cfg")
    column = patch // nz
    z = lax.rem(patch, nz)
    ahead = {"patch": column * nz + lax.rem(z + 1, nz)}
    behind = {"patch": column * nz + lax.rem(z + nz - 1, nz)}
    partner = {"patch": lax.rem(patch + nz, 2 * nz)}
    around = (ahead, behind)
    peers = [{"head": lax.rem(head + i, nh)} for i in range(1, nh)]
    x = lax.rem(head, nx)
    y_hi = head // nx
    opposite = {"head": (1 - y_hi) * nx + x}

    def x_peer(i):
        return {"head": y_hi * nx + lax.rem(x + i, nx)}

    def x_cross(i):
        return {"head": y_hi * nx + lax.rem(x + i, nx), "cfg": 1 - cfg}

    def remote(src, dst, send, recv, device):
        return pltpu.make_async_remote_copy(
            src_ref=src,
            dst_ref=dst,
            send_sem=send,
            recv_sem=recv,
            device_id=device,
            device_id_type=MESH,
        )

    last = nfull * count

    def ring(src, dst, n, side):
        return remote(src, dst, ring_send.at[side, n], ring_recv.at[side, n], around[side])

    def ring_own(k, side):
        return ring(
            stale_ref.at[0, :, :, pl.ds(k * HD, HD)], kv.at[k, :, side], k, side
        )

    def ring_next(u, side):
        return ring(kv.at[u - count, :, side], kv.at[u, :, side], u, side)

    def ring_far(k, part):
        side = 1 if part == 1 or k == 0 else 0
        n = last + 2 * k + part
        return ring(kv.at[last - count + k, part, side], far.at[k, part], n, side)

    def chunk(n, side):
        return ring(kv.at[0, :, side], kv.at[0, :, side], n, side)

    def a2a_to(i):
        target = lax.rem(head + i, nh)
        return remote(
            qkv_ref.at[0, :, :, pl.ds(pl.multiple_of(target * width, HD), width)],
            fresh.at[:, pl.ds(pl.multiple_of(head * tok, tok), tok)],
            a2a_send.at[i],
            a2a_recv.at[i],
            peers[i - 1],
        )

    features = pl.ds(pl.multiple_of(cfg * half, HD), half)
    part_rows = width // 4

    def weight_to(i, j):
        span = pl.ds(j * part_rows, part_rows)
        return remote(
            weight_ref.at[span, features],
            weight.at[x, span],
            weight_send.at[i, j],
            weight_recv.at[i, j],
            x_peer(i),
        )

    own_copy = pltpu.make_async_copy(stale_ref.at[0], own, local_sem.at[0])
    mine_copy = pltpu.make_async_copy(
        qkv_ref.at[0, :, :, pl.ds(pl.multiple_of(head * width, HD), width)],
        fresh.at[:, pl.ds(pl.multiple_of(head * tok, tok), tok)],
        local_sem.at[1],
    )
    weight_copy = pltpu.make_async_copy(
        weight_ref.at[:, features], weight.at[x], local_sem.at[2]
    )
    tokens_copy = pltpu.make_async_copy(tokens_ref, tokens, local_sem.at[3])
    gate_copy = pltpu.make_async_copy(gate_ref, gate, local_sem.at[4])
    next_copy = pltpu.make_async_copy(fresh.at[pl.ds(1, 2)], next_ref.at[0], local_sem.at[5])

    barrier = pltpu.get_barrier_semaphore()
    greeted = [ahead, behind, partner] + peers + [x_cross(i) for i in range(nx)]
    for device in greeted:
        pl.semaphore_signal(barrier, inc=1, device_id=device, device_id_type=MESH)
    own_copy.start()
    mine_copy.start()
    weight_copy.start()
    tokens_copy.start()
    gate_copy.start()
    pl.semaphore_wait(barrier, len(greeted))

    for k in range(count):
        for side in range(2):
            ring_own(k, side).start()
    for i in range(1, nh):
        a2a_to(i).start()

    def pass_on(u):
        for side in range(2):
            chunk(u - count, side).wait_recv()
            ring_next(u, side).start()

    def attend(k, start, size, keys, values, first=False):
        span = pl.ds(start, size)
        scores = lax.dot_general(
            qc[k, span], keys, (((1,), (1,)), ((), ())), preferred_element_type=F32
        )
        block_max = jnp.max(scores, axis=1, keepdims=True)
        if first:
            new_max = jnp.broadcast_to(block_max, (size, HD))
        else:
            old_max = maxima[k, span]
            new_max = jnp.maximum(old_max, block_max)
            factor = jnp.exp2((old_max - new_max) * SCALE2)
        lanes = [
            jnp.exp2((scores[:, j : j + HD] - new_max) * SCALE2)
            for j in range(0, scores.shape[1], HD)
        ]
        total = functools.reduce(jnp.add, lanes)
        weights = jnp.concatenate([lane.astype(BF16) for lane in lanes], axis=1)
        product = jnp.dot(weights, values, preferred_element_type=F32)
        maxima[k, span] = new_max
        if first:
            totals[k, span] = total
            summed[k, span] = product
        else:
            totals[k, span] = totals[k, span] * factor + total
            summed[k, span] = summed[k, span] * factor + product

    def attend_chunk(v):
        k = lax.rem(v, count)
        keys = kv[v, 0].reshape(2 * rows, HD)
        values = kv[v, 1].reshape(2 * rows, HD)
        for start in (0, rows):
            attend(k, start, rows, keys, values)

    def loop(low, high, work):
        def step(i, carry):
            work(i)
            return carry

        lax.fori_loop(low, high, step, 0)

    chunks = nfull * count
    begin = min(3 * count, chunks)
    loop(count, min(2 * count, chunks), pass_on)
    mine_copy.wait()
    for i in range(1, nh):
        a2a_to(i).wait_recv()
    query_copy = remote(
        fresh.at[0], qpart, part_send.at[0, count], part_recv.at[0, count], partner
    )
    query_copy.start()
    next_copy.start()
    for j in range(4):
        for i in range(1, nx):
            weight_to(i, j).start()
    for k in range(count):
        qc[k, 0:rows] = fresh[0, :, k * HD : (k + 1) * HD]
    loop(min(2 * count, chunks), begin, pass_on)
    own_copy.wait()
    query_copy.wait_recv()
    for k in range(count):
        columns = slice(k * HD, (k + 1) * HD)
        qc[k, rows : 2 * rows] = qpart[:, columns]
        attend(k, 0, rows, fresh[1, :, columns], fresh[2, :, columns], first=True)
        attend(k, rows, rows, own[0, :, columns], own[1, :, columns], first=True)

    double = max(0, min(chunks - begin, begin - count))

    def catch_up(i):
        pass_on(begin + i)
        loop(2 * i, 2 * i + 2, attend_chunk)

    def follow(u):
        pass_on(u)
        attend_chunk(u - count)

    loop(0, double, catch_up)
    loop(begin + double, chunks, follow)
    done = 2 * double + max(0, chunks - begin - double)
    loop(done, chunks - count, attend_chunk)
    for k in range(count):
        u = chunks - count + k
        for side in range(2):
            chunk(u, side).wait_recv()
        for part in range(2):
            ring_far(k, part).start()
        attend_chunk(u)

    def part_copy(k):
        return remote(
            part_out.at[k], part_in.at[k], part_send.at[0, k], part_recv.at[0, k], partner
        )

    def stat_copy(k):
        return remote(
            stat_out.at[k], stat_in.at[k], part_send.at[1, k], part_recv.at[1, k], partner
        )

    crossing = [(1, i) for i in range(nx)] + [(0, i) for i in range(1, nx)]

    def tile_copy(k, flip, i):
        return remote(
            att.at[k, :, lax.rem(x + i, nx)],
            tiles.at[k, cfg, x],
            tile_send.at[k, flip, i],
            tile_recv.at[k, flip, i],
            x_cross(i) if flip else x_peer(i),
        )

    lane = lax.broadcasted_iota(jnp.int32, (rows, HD), 1)
    for k in range(count):
        for side in range(2):
            ring_far(k, side).wait_recv()
        attend(k, rows, rows, far[k, 0], far[k, 1])
        total = jnp.sum(totals[k, rows : 2 * rows], axis=1, keepdims=True)
        stats = jnp.where(lane < 4, maxima[k, rows : 2 * rows], total)
        stat_out[k] = jnp.transpose(stats)[0:8]
        stat_copy(k).start()
        part_out[k] = summed[k, rows : 2 * rows].astype(BF16)
        part_copy(k).start()
        attend(k, 0, rows, far[k, 0], far[k, 1])

    for k in range(count):
        max_here = maxima[k, 0:rows]
        total_here = jnp.sum(totals[k, 0:rows], axis=1, keepdims=True)
        stat_copy(k).wait_recv()
        max_there = jnp.transpose(jnp.broadcast_to(stat_in[k, 0:1], (HD, rows)))
        total_there = jnp.transpose(jnp.broadcast_to(stat_in[k, 4:5], (HD, rows)))
        top = jnp.maximum(max_here, max_there)
        keep = jnp.exp2((max_here - top) * SCALE2)
        add = jnp.exp2((max_there - top) * SCALE2)
        total = total_here * keep + total_there * add
        part_copy(k).wait_recv()
        value = summed[k, 0:rows] * keep + part_in[k].astype(F32) * add
        att[k] = (value / total).astype(BF16).reshape(2, nx, tok, HD)
        for flip, i in crossing:
            tile_copy(k, flip, i).start()
        tiles[k, cfg, x] = att[k, :, x]

    weight_copy.wait()
    for i in range(1, nx):
        for j in range(4):
            weight_to(i, j).wait_recv()
    tokens_copy.wait()
    gate_copy.wait()
    piece = 512 if half % 512 == 0 else half
    pieces = half // piece

    def rs_copy(j):
        columns = pl.ds(j * piece, piece)
        return remote(
            rs_out.at[:, columns], rs_in.at[:, columns], rs_send.at[j], rs_recv.at[j], opposite
        )

    for k in range(count):
        for flip, i in crossing:
            tile_copy(k, flip, i).wait_recv()
        both = GUIDE * tiles[k, 0].astype(F32) + (1.0 - GUIDE) * tiles[k, 1].astype(F32)
        both = both.astype(BF16)
        table = jnp.concatenate([both[i].reshape(2 * tok, HD) for i in range(nx)], axis=1)
        for j in range(pieces):
            columns = pl.ds(j * piece, piece)
            factors = weight[:, k * HD : (k + 1) * HD, columns].reshape(nx * HD, piece)
            result = jnp.dot(table, factors, preferred_element_type=F32)
            result = result.reshape(2, tok, piece)
            if k == 0:
                sums[:, :, columns] = result
            else:
                sums[:, :, columns] += result
            if k == count - 1:
                rs_out[:, columns] = sums[1 - y_hi, :, columns].astype(BF16)
                rs_copy(j).start()
    next_copy.wait()
    query_copy.wait_send()

    def sent(n):
        for side in range(2):
            chunk(n, side).wait_send()

    loop(0, last, sent)
    for k in range(count):
        for side in range(2):
            ring_far(k, side).wait_send()
        part_copy(k).wait_send()
        stat_copy(k).wait_send()
        for flip, i in crossing:
            tile_copy(k, flip, i).wait_send()
    for i in range(1, nh):
        a2a_to(i).wait_send()
    for i in range(1, nx):
        for j in range(4):
            weight_to(i, j).wait_send()
    for j in range(pieces):
        columns = pl.ds(j * piece, piece)
        rs_copy(j).wait_recv()
        value = sums[y_hi, :, columns] + rs_in[:, columns].astype(F32)
        scaled = gate[columns].reshape(1, piece) * value
        guided_ref[:, columns] = (tokens[:, columns].astype(F32) + scaled).astype(BF16)
    for j in range(pieces):
        rs_copy(j).wait_send()


def solution(mesh):
    nz = mesh.shape["patch"] // 2
    nh = mesh.shape["head"]

    def body(qkv, stale_kv, tokens_in, out_weight, gate):
        tok = qkv.shape[2]
        rows = tok * nh
        width = stale_kv.shape[3]
        count = width // HD
        half = tokens_in.shape[1]
        nx = nh // 2
        nfull = nz // 2 - 1
        pieces = half // 512 if half % 512 == 0 else 1
        anywhere = pl.BlockSpec(memory_space=pl.ANY)
        dma = pltpu.SemaphoreType.DMA
        return pl.pallas_call(
            functools.partial(kernel, nz, nh),
            out_shape=(
                pltpu.VMEM((1, 2, rows, width), BF16),
                pltpu.VMEM((tok, half), BF16),
            ),
            in_specs=[anywhere] * 5,
            out_specs=(pl.BlockSpec(memory_space=pltpu.VMEM),) * 2,
            scratch_shapes=[
                pltpu.VMEM((3, rows, width), BF16),
                pltpu.VMEM((2, rows, width), BF16),
                pltpu.VMEM((nfull * count, 2, 2, rows, HD), BF16),
                pltpu.VMEM((count, 2, rows, HD), BF16),
                pltpu.VMEM((count, 2 * rows, HD), BF16),
                pltpu.VMEM((rows, width), BF16),
                pltpu.VMEM((count, 2 * rows, HD), F32),
                pltpu.VMEM((count, 2 * rows, HD), F32),
                pltpu.VMEM((count, 2 * rows, HD), F32),
                pltpu.VMEM((count, rows, HD), BF16),
                pltpu.VMEM((count, rows, HD), BF16),
                pltpu.VMEM((count, 8, rows), F32),
                pltpu.VMEM((count, 8, rows), F32),
                pltpu.VMEM((count, 2, nx, tok, HD), BF16),
                pltpu.VMEM((count, 2, nx, 2, tok, HD), BF16),
                pltpu.VMEM((nx, width, half), BF16),
                pltpu.VMEM((tok, half), BF16),
                pltpu.VMEM((half,), F32),
                pltpu.VMEM((2, tok, half), F32),
                pltpu.VMEM((tok, half), BF16),
                pltpu.VMEM((tok, half), BF16),
                dma((2, (nfull + 2) * count)),
                dma((2, (nfull + 2) * count)),
                dma((nh,)),
                dma((nh,)),
                dma((2, count + 1)),
                dma((2, count + 1)),
                dma((count, 2, nx)),
                dma((count, 2, nx)),
                dma((nx, 4)),
                dma((nx, 4)),
                dma((pieces,)),
                dma((pieces,)),
                dma((6,)),
            ],
            compiler_params=pltpu.CompilerParams(
                collective_id=0, has_side_effects=True, vmem_limit_bytes=62 * 1024 * 1024
            ),
        )(qkv, stale_kv, tokens_in, out_weight, gate)

    in_specs = (
        P("cfg", None, ("patch", "head"), None),
        P("cfg", None, "patch", "head"),
        P(("patch", "head"), "cfg"),
        P("head", None),
        P("cfg"),
    )
    out_specs = (P("cfg", None, "patch", "head"), P(("patch", "head"), "cfg"))
    return jax.shard_map(body, mesh=mesh, in_specs=in_specs, out_specs=out_specs, check_vma=False)
```
